512 devices in a mesh: depth: 2 (over x_lo), row: 16 (over x_hi, z), col: 16 (over y, core).
Axes of the slice: x: 4 (x_hi: 2, x_lo: 2; x = x_hi * 2 + x_lo), y: 8, z: 8, core: 2. Of those that a mesh axis runs over, the one named last changes fastest.
Arguments:
- context: bfloat16 [4096, 12288], P(('depth', 'row'), 'col'), may hold values from -6 to 6
- d_out: bfloat16 [4096, 12288], P(('depth', 'col'), 'row'), may hold values from -6 to 6
- out_weight: bfloat16 [12288, 12288], P('col', 'row'), may hold values from -0.0546875 to 0.0546875
Outputs:
- d_context: bfloat16 [4096, 12288], P(('depth', 'row'), 'col')
- d_weight: bfloat16 [12288, 12288], P('col', 'row')
The draws below stay inside these ranges and needn't reach their ends.
All inputs are finite; a program needn't handle non-finite values.
Results may differ from the reference program's by a relative error of at most 0.02.
Values may be sent and summed in bfloat16 or wider, within the bound.
No kernel may reach another device: no remote copies, remote signals or barrier semaphores. Data moves between devices by JAX's collectives and lax.ppermute only.
A program may use at most 64 MiB of HBM per device.

```python
import jax
import jax.numpy as jnp
from jax import lax

D = 12288
DI = 12288
TOKENS = 4096
N_ROW = 16


def spiked(result, own_key, source, target, blocks, factor):
    def block_of(axis_at):
        return (jnp.arange(result.shape[axis_at]) // (result.shape[axis_at] // blocks)).reshape((-1,) + (1,) * (result.ndim - 1 - axis_at))

    one_side = jax.random.permutation(own_key, blocks)[block_of(target)]
    second = (block_of(target) + blocks // 2) % blocks
    return jnp.where((block_of(source) == one_side) | (block_of(source) == second), factor * result, result)


def block_levels(own_key, extent, split, low, high):
    factor_of, own = 1.0, jax.random.fold_in(own_key, 6)
    for position, parts in split:
        steps = jnp.exp(jax.random.uniform(jax.random.fold_in(own, position), (parts,), jnp.float32, low / len(split), high / len(split)))
        factor_of = factor_of * jnp.repeat(steps, extent[position] // parts).reshape([-1 if axis == position else 1 for axis in range(len(extent))])
    return factor_of


def normal_values(stream_key, shape, width, most, pieces=(), kind=jnp.bfloat16):
    values = jax.random.normal(stream_key, shape, jnp.float32) * width
    if len(pieces) > 0:
        values = block_levels(stream_key, shape, pieces, -0.22, 0.18) * values
    return jnp.clip(values, min=-most, max=most).astype(kind)


def gaussian_with(own_key, extent, width, limit, cuts, heavy, kind=jnp.bfloat16):
    values = width * jax.random.normal(own_key, extent, jnp.float32)
    if cuts:
        values = values * block_levels(own_key, extent, cuts, -0.22, 0.18)
    return jnp.clip(spiked(values, jax.random.fold_in(own_key, 3), *heavy), -limit, limit).astype(kind)


def setup_inputs(seed: int = 0) -> dict:
    seeds = jax.random.split(jax.random.key(seed), 4)
    return {
        "context": normal_values(seeds[0], (TOKENS, DI), 1.0, 6.0, ((0, 32), (1, 16))),
        "d_out": gaussian_with(seeds[1], (TOKENS, D), 1.0, 6.0, ((0, 32), (1, 16)), (1, 0, 32, 2.75)),
        "out_weight": normal_values(seeds[2], (DI, D), D ** -0.5, 0.0546875, ((0, 16), (1, 16))),
    }


def reference(context, d_out, out_weight):
    block = D // N_ROW

    def add_block(total, index):
        start = (index * block).astype(jnp.int32)
        grad_piece = lax.dynamic_slice_in_dim(d_out, start, block, 1)
        weight_piece = lax.dynamic_slice_in_dim(out_weight, start, block, 1)
        partial_value = lax.dot_general(grad_piece, weight_piece, (((1,), (1,)), ((), ())), preferred_element_type=jnp.float32)
        return total + partial_value.astype(jnp.bfloat16).astype(jnp.float32), None

    empty = jnp.zeros((d_out.shape[0], out_weight.shape[0]), jnp.float32)
    d_context, unused = lax.scan(add_block, empty, jnp.arange(N_ROW, dtype=jnp.int32))
    d_weight = lax.dot_general(context, d_out, (((0,), (0,)), ((), ())), preferred_element_type=jnp.float32)
    return d_context.astype(jnp.bfloat16), d_weight.astype(jnp.bfloat16)
```

```python
import jax
import jax.numpy as jnp
from jax import lax
from jax.experimental import pallas as pl
from jax.experimental.pallas import tpu as pltpu
from jax.sharding import PartitionSpec as P

X_HI = 2
Z = 8
Y = 8
CORES = 2
F32 = jnp.float32
BF16 = jnp.bfloat16

X_SWAP = [(i, (i + Z) % (X_HI * Z)) for i in range(X_HI * Z)]
CORE_SWAP = [(i, i ^ 1) for i in range(Y * CORES)]


def along_z(block, step):
    pairs = [(h * Z + z, h * Z + (z + step) % Z) for h in range(X_HI) for z in range(Z)]
    return lax.ppermute(block, "row", pairs)


def x_swap(block):
    return lax.ppermute(block, "row", X_SWAP)


def ring(block, other_x=0, other_core=0):
    pairs = []
    for h in range(X_HI):
        for z in range(Z):
            for y in range(Y):
                for k in range(CORES):
                    to_row = (h ^ other_x) * Z + (z + 1 - 2 * k) % Z
                    source = (h * Z + z) * Y * CORES + y * CORES + k
                    pairs.append((source, to_row * Y * CORES + y * CORES + (k ^ other_core)))
    return lax.ppermute(block, ("row", "col"), pairs)


def weight_kernel(places, *refs):
    *pieces, grad, out, total = refs
    found = [(ref, i) for ref in pieces for i in range(ref.shape[0])]
    for n in range(0, len(found), 2):
        left = jnp.concatenate([ref[i] for ref, i in found[n : n + 2]])
        right = jnp.concatenate([grad[places[n + i]] for i in range(2)])
        term = lax.dot_general(left, right, (((0,), (0,)), ((), ())), preferred_element_type=F32)
        if n == 0:
            total[...] = term
        else:
            total[...] += term
    out[...] = total[...].astype(BF16)


def weight_sum(places, pieces, grad):
    shape = (pieces[0].shape[-1], grad.shape[-1])
    in_vmem = pl.BlockSpec(memory_space=pltpu.VMEM)
    return pl.pallas_call(
        weight_kernel,
        out_shape=jax.ShapeDtypeStruct(shape, BF16),
        in_specs=[pl.BlockSpec(memory_space=pltpu.SMEM)] + [in_vmem] * (len(pieces) + 1),
        out_specs=in_vmem,
        scratch_shapes=[pltpu.VMEM(shape, F32)],
        compiler_params=pltpu.CompilerParams(vmem_limit_bytes=40 * 2**20),
        cost_estimate=pl.CostEstimate(
            flops=2 * grad.size * shape[0], bytes_accessed=4 * grad.size, transcendentals=0
        ),
        name="weight_sum",
    )(places, *pieces, grad)


def on_device(context, d_out, out_weight):
    rows, features = d_out.shape
    row, col = lax.axis_index("row"), lax.axis_index("col")
    h, z = row // Z, row % Z
    core = col % CORES
    together = lax.optimization_barrier

    grad_rows = lax.all_gather(d_out, "col", axis=0, tiled=True)

    context = context[None]
    pair = jnp.concatenate([context, along_z(context, 4)])
    weights = (out_weight, lax.ppermute(out_weight, "col", CORE_SWAP))
    pair, weights = together((pair, weights))
    up, down, x_pair = along_z(pair, 1), along_z(pair, -1), x_swap(pair)
    up, down, x_pair = together((up, down, x_pair))
    four = jnp.concatenate([up, down])
    x_four = x_swap(four)
    two = jnp.concatenate([along_z(up[:1], 1), along_z(down[:1], -1)])
    distances = jnp.array([0, 4, 7, 3, 1, 5, 6, 2])
    places = jnp.concatenate([side * Z + (z + distances) % Z for side in (h, 1 - h)])

    grad_rows, two = together((grad_rows, two))
    x_two = x_swap(two)
    blocks = grad_rows.reshape(X_HI, Z, rows, features)

    def tokens(step, x_hi=None):
        at = (z + (1 - 2 * core) * step + Z) % Z
        start = (0 if x_hi is None else x_hi, at, 0, 0)
        return lax.dynamic_slice(blocks, start, (X_HI if x_hi is None else 1, 1, rows, features))[:, 0]

    def product(grad, weight):
        return lax.dot_general(
            grad, weight, (((grad.ndim - 1,), (1,)), ((), ())), preferred_element_type=F32
        ).astype(BF16)

    half = (jnp.arange(X_HI) == core)[:, None, None]
    first = tokens(4, core)
    sums = [ring(product(first, w)) for w in weights]
    rest = jnp.stack([tokens(step) for step in (1, 2, 3)])
    partials = [product(rest, w) for w in weights]
    own = product(tokens(0), out_weight)
    keep = lax.dynamic_index_in_dim(own, h, 0, False)
    send = lax.dynamic_index_in_dim(own, 1 - h, 0, False)
    sums, partials, keep, send, x_four = together((sums, partials, keep, send, x_four))
    sums = [
        ring((p[2].astype(F32) + jnp.where(half, s.astype(F32), 0.0)).astype(BF16))
        for p, s in zip(partials, sums)
    ]

    pieces = [pair, four, two, x_pair, x_four, x_two]
    partial_weight = weight_sum(places, pieces, grad_rows.reshape(-1, rows, features))
    other_weight = lax.ppermute(partial_weight, "depth", [(0, 1), (1, 0)])

    sums, unused = together((sums, partial_weight))
    sums = [ring((p[1].astype(F32) + s.astype(F32)).astype(BF16)) for p, s in zip(partials, sums)]
    terms = [keep, x_swap(send)]
    sums, terms = together((sums, terms))
    for other_core, (p, s) in enumerate(zip(partials, sums)):
        last = (p[0].astype(F32) + s.astype(F32)).astype(BF16)
        for other_x in range(X_HI):
            part = lax.dynamic_index_in_dim(last, h ^ other_x, 0, False)
            terms.append(ring(part, other_x, other_core))
    d_context = sum(t.astype(F32) for t in terms).astype(BF16)
    d_weight = (partial_weight.astype(F32) + other_weight.astype(F32)).astype(BF16)
    return (d_context, d_weight)


def solution(mesh):
    in_specs = (P(("depth", "row"), "col"), P(("depth", "col"), "row"), P("col", "row"))
    out_specs = (P(("depth", "row"), "col"), P("col", "row"))
    return jax.shard_map(
        on_device, mesh=mesh, in_specs=in_specs, out_specs=out_specs, check_vma=False
    )
```

```python
import functools

import jax
import jax.numpy as jnp
from jax import lax
from jax.experimental import pallas as pl
from jax.experimental.pallas import tpu as pltpu
from jax.sharding import PartitionSpec as P

X_HI = 2
Z = 8
Y = 8
CORES = 2
PARTS = 2
F32 = jnp.float32
BF16 = jnp.bfloat16
F16 = jnp.float16
POWERS = [12 + 8 * n for n in range(15)]
TAG_ROWS = 16

Z_GROUPS = [[h * Z + z for z in range(Z)] for h in range(X_HI)]
X_SWAP = [(i, (i + Z) % (X_HI * Z)) for i in range(X_HI * Z)]
CORE_SWAP = [(i, i ^ 1) for i in range(Y * CORES)]
IN_VMEM = pl.BlockSpec(memory_space=pltpu.VMEM)
IN_SMEM = pl.BlockSpec(memory_space=pltpu.SMEM)


def scale_kernel(block, out):
    rows = block.shape[0]
    wide = block[...].astype(F32)
    largest = jnp.max(jnp.max(jnp.abs(wide), axis=0, keepdims=True), axis=1, keepdims=True)
    n, scale = jnp.zeros((1, 1), F32), jnp.full((1, 1), 2.0 ** POWERS[0], F32)
    for power in POWERS[1:]:
        small = largest < 2.0 ** (15 - power)
        n = jnp.where(small, n + 1, n)
        scale = jnp.where(small, F32(2.0**power), scale)
    out[:rows] = (wide * scale).astype(BF16)
    out[rows:] = jnp.broadcast_to(n, (TAG_ROWS, block.shape[1])).astype(BF16)


def gather_grad(d_out):
    rows, features = d_out.shape
    (sent,) = local_call(
        scale_kernel,
        [(rows + TAG_ROWS, features)],
        0,
        in_specs=[IN_VMEM],
        out_specs=[IN_VMEM],
        name="scale_block",
    )(d_out)
    return lax.all_gather(sent.astype(F16), "col", axis=0, tiled=True)


def scaled_back(found, rows):
    found = found.reshape(-1, rows + TAG_ROWS, found.shape[1])
    n = found[:, rows, 0].astype(F32)
    back = sum(jnp.where(n == i, F32(2.0**-power), F32(0)) for i, power in enumerate(POWERS))
    return (found[:, :rows].astype(F32) * back[:, None, None]).astype(BF16)


def core_swap(block):
    return lax.ppermute(block, "col", CORE_SWAP)


def x_swap(block):
    return lax.ppermute(block, "row", X_SWAP)


def ring(block, other_x=0, other_core=0, chips=1):
    pairs = []
    for h in range(X_HI):
        for z in range(Z):
            for y in range(Y):
                for k in range(CORES):
                    to_row = (h ^ other_x) * Z + (z + chips * (1 - 2 * k)) % Z
                    source = (h * Z + z) * Y * CORES + y * CORES + k
                    pairs.append((source, to_row * Y * CORES + y * CORES + (k ^ other_core)))
    return lax.ppermute(block, ("row", "col"), pairs)


def local_call(kernel, shapes, flops, **options):
    return pl.pallas_call(
        kernel,
        out_shape=[jax.ShapeDtypeStruct(shape, BF16) for shape in shapes],
        compiler_params=pltpu.CompilerParams(vmem_limit_bytes=40 * 2**20),
        cost_estimate=pl.CostEstimate(flops=flops, bytes_accessed=2**23, transcendentals=0),
        **options,
    )


def dot(grad, weight):
    return lax.dot_general(grad, weight, (((1,), (1,)), ((), ())), preferred_element_type=F32)


def spread_kernel(block, out):
    for i in range(out.shape[0]):
        out[i] = block[...]


def first_kernel(places, here, there, far, partner, weight, other_weight, out, far_out, partner_out):
    rows, width = here.shape[1], weight.shape[0]
    grad = jnp.concatenate([here[0], there[0], far[0], partner[0]])
    found = dot(grad, weight[...]).astype(BF16)
    partner_out[...] = found[3 * rows :]
    for i in range(CORES):
        if i == 1:
            found = dot(grad[: 3 * rows], other_weight[...]).astype(BF16)
        cut = slice(i * width, (i + 1) * width)
        out[0, :, cut] = found[:rows]
        out[1, :, cut] = found[rows : 2 * rows]
        far_out[:, cut] = found[2 * rows : 3 * rows]


def pack_kernel(context, out):
    out[...] = context[:, :, : out.shape[2]]


def last_kernel(context, partner, out):
    part = out.shape[2]
    out[:Z] = context[:, :, -part:]
    for i in range(PARTS):
        out[Z + i] = partner[:, i * part : (i + 1) * part]


def near_kernel(places, grad, weight, other_weight, *outs):
    *steps, own = outs
    rows, width = grad.shape[1], weight.shape[0]
    for n, out in enumerate(steps):
        both = jnp.concatenate([grad[places[n * X_HI + i]] for i in range(X_HI)])
        for j, w in enumerate((weight, other_weight)):
            found = dot(both, w[...]).astype(BF16)
            for i in range(X_HI):
                out[i, :, j * width : (j + 1) * width] = found[i * rows : (i + 1) * rows]
    own[...] = dot(grad[places[X_HI * len(steps)]], weight[...]).astype(BF16)


def join_kernel(at, part, arrived, far, out):
    other = 1 - at[0]
    total = part[at[0]].astype(F32) + arrived[at[0]].astype(F32) + far[...].astype(F32)
    out[at[0]] = total.astype(BF16)
    out[other] = (part[other].astype(F32) + arrived[other].astype(F32)).astype(BF16)


def weight_kernel(part, x_hi, near, across, grad, out, total):
    width = out.shape[0]
    for other_x, context in enumerate((near, across)):
        cut = slice(part * width, (part + 1) * width) if other_x == 0 else slice(0, width)
        for z in range(0, Z, 2):
            left = jnp.concatenate([context[z + i, :, cut] for i in range(2)])
            at = (x_hi[0] ^ other_x) * Z + z
            right = jnp.concatenate([grad[at + i] for i in range(2)])
            term = lax.dot_general(left, right, (((0,), (0,)), ((), ())), preferred_element_type=F32)
            if other_x == 0 and z == 0:
                total[...] = term
            else:
                total[...] += term
    out[...] = total[...].astype(BF16)


def on_device(context, d_out, out_weight):
    rows, features = d_out.shape
    width = out_weight.shape[0]
    row, col = lax.axis_index("row"), lax.axis_index("col")
    h, z = row // Z, row % Z
    core = col % CORES
    together = lax.optimization_barrier

    (spread,) = local_call(
        spread_kernel,
        [(Z, rows, width)],
        0,
        in_specs=[IN_VMEM],
        out_specs=[IN_VMEM],
        name="spread_context",
    )(context)
    near = lax.all_to_all(spread, "row", 0, 0, tiled=True, axis_index_groups=Z_GROUPS)
    weights = (out_weight, core_swap(out_weight))
    found = gather_grad(d_out)
    part = width // PARTS
    (packed,) = local_call(
        pack_kernel,
        [(Z, rows, part)],
        0,
        in_specs=[IN_VMEM],
        out_specs=[IN_VMEM],
        name="pack_context",
    )(near)
    found, packed = together((found, packed))
    across = [x_swap(packed)]
    grad = scaled_back(found, rows)

    def place(step, other_x):
        return (h ^ other_x) * Z + (z + (1 - 2 * core) * step + Z) % Z

    def add(a, b):
        return (a.astype(F32) + b.astype(F32)).astype(BF16)

    block_flops = 2 * rows * features * width
    two_blocks = (X_HI, rows, CORES * width)
    far_x = h ^ core
    total, far, partner = local_call(
        first_kernel,
        [two_blocks, two_blocks[1:], (rows, width)],
        7 * block_flops,
        grid_spec=pltpu.PrefetchScalarGridSpec(
            num_scalar_prefetch=1,
            grid=(1,),
            in_specs=[
                pl.BlockSpec((1, rows, features), lambda i, places, n=n: (places[n], 0, 0))
                for n in range(4)
            ]
            + [IN_VMEM] * 2,
            out_specs=[IN_VMEM] * 3,
        ),
        name="first_products",
    )(
        jnp.stack([place(3, 0), place(3, 1), place(4, far_x), place(0, 1)]), *[grad] * 4, *weights
    )
    (packed,) = local_call(
        last_kernel,
        [(Z + PARTS, rows, part)],
        0,
        in_specs=[IN_VMEM] * 2,
        out_specs=[IN_VMEM],
        name="pack_last",
    )(near, partner)
    across.append(x_swap(packed))
    total, far = ring(total), ring(far, chips=2)
    *parts, own = local_call(
        near_kernel,
        [two_blocks] * 2 + [(rows, width)],
        9 * block_flops,
        in_specs=[IN_SMEM] + [IN_VMEM] * 3,
        out_specs=[IN_VMEM] * 3,
        name="near_products",
    )(
        jnp.stack([place(step, i) for step in (2, 1) for i in range(X_HI)] + [place(0, 0)]),
        grad,
        *weights,
    )
    terms = [own, jnp.concatenate([across[1][Z + i] for i in range(PARTS)], axis=1)]
    total, far, across[0] = together((total, far, across[0]))
    (total,) = local_call(
        join_kernel,
        [two_blocks],
        0,
        in_specs=[IN_SMEM] + [IN_VMEM] * 3,
        out_specs=[IN_VMEM],
        name="join_sums",
    )(far_x[None], parts[0], total, far)
    total = ring(total)

    weight_sums = []
    for i in range(PARTS):
        shape = (width // PARTS, features)
        weight_sums += local_call(
            functools.partial(weight_kernel, i),
            [shape],
            16 * block_flops // PARTS,
            in_specs=[IN_SMEM] + [IN_VMEM] * 3,
            out_specs=[IN_VMEM],
            scratch_shapes=[pltpu.VMEM(shape, F32)],
            name="weight_sum",
        )(h[None], near, across[i], grad)
    other_sums = [lax.ppermute(part, "depth", [(0, 1), (1, 0)]) for part in weight_sums]

    total, unused = together((total, weight_sums))
    last = add(parts[1], total)
    for other_x in range(X_HI):
        terms += [
            ring(last[other_x, :, i * width : (i + 1) * width], other_x, i) for i in range(CORES)
        ]
    terms, other_sums = together((terms, other_sums))
    d_context = sum(t.astype(F32) for t in terms).astype(BF16)
    d_weight = jnp.concatenate([add(*part) for part in zip(weight_sums, other_sums)])
    return (d_context, d_weight)


def solution(mesh):
    in_specs = (P(("depth", "row"), "col"), P(("depth", "col"), "row"), P("col", "row"))
    out_specs = (P(("depth", "row"), "col"), P("col", "row"))
    return jax.shard_map(
        on_device, mesh=mesh, in_specs=in_specs, out_specs=out_specs, check_vma=False
    )
```

```python
import functools

import jax
import jax.numpy as jnp
from jax import lax
from jax.experimental import pallas as pl
from jax.experimental.pallas import tpu as pltpu
from jax.sharding import PartitionSpec as P

X_HI = 2
Z = 8
Y = 8
CORES = 2
PARTS = 2
F32 = jnp.float32
BF16 = jnp.bfloat16
F16 = jnp.float16
POWERS = [12 + 8 * n for n in range(15)]
TAG_ROWS = 16

Z_GROUPS = [[h * Z + z for z in range(Z)] for h in range(X_HI)]
X_SWAP = [(i, (i + Z) % (X_HI * Z)) for i in range(X_HI * Z)]
CORE_SWAP = [(i, i ^ 1) for i in range(Y * CORES)]
IN_VMEM = pl.BlockSpec(memory_space=pltpu.VMEM)
IN_SMEM = pl.BlockSpec(memory_space=pltpu.SMEM)


def scale_kernel(block, out):
    rows = block.shape[0]
    wide = block[...].astype(F32)
    largest = jnp.max(jnp.max(jnp.abs(wide), axis=0, keepdims=True), axis=1, keepdims=True)
    n, scale = jnp.zeros((1, 1), F32), jnp.full((1, 1), 2.0 ** POWERS[0], F32)
    for power in POWERS[1:]:
        small = largest < 2.0 ** (15 - power)
        n = jnp.where(small, n + 1, n)
        scale = jnp.where(small, F32(2.0**power), scale)
    out[:rows] = (wide * scale).astype(BF16)
    out[rows:] = jnp.broadcast_to(n, (TAG_ROWS, block.shape[1])).astype(BF16)


def gather_grad(d_out):
    rows, features = d_out.shape
    (sent,) = local_call(
        scale_kernel,
        [(rows + TAG_ROWS, features)],
        0,
        in_specs=[IN_VMEM],
        out_specs=[IN_VMEM],
        name="scale_block",
    )(d_out)
    return lax.all_gather(sent.astype(F16), "col", axis=0, tiled=True)


def scaled_back(found, rows):
    found = found.reshape(-1, rows + TAG_ROWS, found.shape[1])
    n = found[:, rows, 0].astype(F32)
    back = sum(jnp.where(n == i, F32(2.0**-power), F32(0)) for i, power in enumerate(POWERS))
    return (found[:, :rows].astype(F32) * back[:, None, None]).astype(BF16)


def core_swap(block):
    return lax.ppermute(block, "col", CORE_SWAP)


def x_swap(block):
    return lax.ppermute(block, "row", X_SWAP)


def ring(block, other_x=0, other_core=0, chips=1):
    pairs = []
    for h in range(X_HI):
        for z in range(Z):
            for y in range(Y):
                for k in range(CORES):
                    to_row = (h ^ other_x) * Z + (z + chips * (1 - 2 * k)) % Z
                    source = (h * Z + z) * Y * CORES + y * CORES + k
                    pairs.append((source, to_row * Y * CORES + y * CORES + (k ^ other_core)))
    return lax.ppermute(block, ("row", "col"), pairs)


def local_call(kernel, shapes, flops, **options):
    return pl.pallas_call(
        kernel,
        out_shape=[jax.ShapeDtypeStruct(shape, BF16) for shape in shapes],
        compiler_params=pltpu.CompilerParams(vmem_limit_bytes=40 * 2**20),
        cost_estimate=pl.CostEstimate(flops=flops, bytes_accessed=2**23, transcendentals=0),
        **options,
    )


def dot(grad, weight):
    return lax.dot_general(grad, weight, (((1,), (1,)), ((), ())), preferred_element_type=F32)


def spread_kernel(block, out):
    for i in range(out.shape[0]):
        out[i] = block[...]


def first_kernel(places, here, there, far, partner, weight, other_weight, out, far_out, partner_out):
    rows, width = here.shape[1], weight.shape[0]
    grad = jnp.concatenate([here[0], there[0], far[0], partner[0]])
    found = dot(grad, weight[...]).astype(BF16)
    partner_out[...] = found[3 * rows :]
    for i in range(CORES):
        if i == 1:
            found = dot(grad[: 3 * rows], other_weight[...]).astype(BF16)
        cut = slice(i * width, (i + 1) * width)
        out[0, :, cut] = found[:rows]
        out[1, :, cut] = found[rows : 2 * rows]
        far_out[:, cut] = found[2 * rows : 3 * rows]


def last_kernel(context, partner, out):
    part = out.shape[2]
    out[:Z] = context[:, :, -part:]
    for i in range(PARTS):
        out[Z + i] = partner[:, i * part : (i + 1) * part]


def near_kernel(places, grad, weight, other_weight, *outs):
    *steps, own = outs
    rows, width = grad.shape[1], weight.shape[0]
    for n, out in enumerate(steps):
        both = jnp.concatenate([grad[places[n * X_HI + i]] for i in range(X_HI)])
        for j, w in enumerate((weight, other_weight)):
            found = dot(both, w[...]).astype(BF16)
            for i in range(X_HI):
                out[i, :, j * width : (j + 1) * width] = found[i * rows : (i + 1) * rows]
    own[...] = dot(grad[places[X_HI * len(steps)]], weight[...]).astype(BF16)


def join_kernel(at, part, arrived, far, out):
    other = 1 - at[0]
    total = part[at[0]].astype(F32) + arrived[at[0]].astype(F32) + far[...].astype(F32)
    out[at[0]] = total.astype(BF16)
    out[other] = (part[other].astype(F32) + arrived[other].astype(F32)).astype(BF16)


def weight_kernel(part, x_hi, near, across, grad, out, total):
    width = out.shape[0]
    for other_x, context in enumerate((near, across)):
        cut = slice(part * width, (part + 1) * width) if other_x == 0 else slice(0, width)
        for z in range(0, Z, 2):
            left = jnp.concatenate([context[z + i, :, cut] for i in range(2)])
            at = (x_hi[0] ^ other_x) * Z + z
            right = jnp.concatenate([grad[at + i] for i in range(2)])
            term = lax.dot_general(left, right, (((0,), (0,)), ((), ())), preferred_element_type=F32)
            if other_x == 0 and z == 0:
                total[...] = term
            else:
                total[...] += term
    out[...] = total[...].astype(BF16)


def on_device(context, d_out, out_weight):
    rows, features = d_out.shape
    width = out_weight.shape[0]
    row, col = lax.axis_index("row"), lax.axis_index("col")
    h, z = row // Z, row % Z
    core = col % CORES
    together = lax.optimization_barrier

    (spread,) = local_call(
        spread_kernel,
        [(Z, rows, width)],
        0,
        in_specs=[IN_VMEM],
        out_specs=[IN_VMEM],
        name="spread_context",
    )(context)
    near = lax.all_to_all(spread, "row", 0, 0, tiled=True, axis_index_groups=Z_GROUPS)
    found, out_weight = together((gather_grad(d_out), out_weight))
    weights = (out_weight, core_swap(out_weight))
    grad, near = together((scaled_back(found, rows), near))
    part = width // PARTS
    packed = near[:, :, :part]
    grad, packed = together((grad, packed))
    across = [x_swap(packed)]

    def place(step, other_x):
        return (h ^ other_x) * Z + (z + (1 - 2 * core) * step + Z) % Z

    def add(a, b):
        return (a.astype(F32) + b.astype(F32)).astype(BF16)

    block_flops = 2 * rows * features * width
    two_blocks = (X_HI, rows, CORES * width)
    far_x = h ^ core
    total, far, partner = local_call(
        first_kernel,
        [two_blocks, two_blocks[1:], (rows, width)],
        7 * block_flops,
        grid_spec=pltpu.PrefetchScalarGridSpec(
            num_scalar_prefetch=1,
            grid=(1,),
            in_specs=[
                pl.BlockSpec((1, rows, features), lambda i, places, n=n: (places[n], 0, 0))
                for n in range(4)
            ]
            + [IN_VMEM] * 2,
            out_specs=[IN_VMEM] * 3,
        ),
        name="first_products",
    )(
        jnp.stack([place(3, 0), place(3, 1), place(4, far_x), place(0, 1)]), *[grad] * 4, *weights
    )
    (packed,) = local_call(
        last_kernel,
        [(Z + PARTS, rows, part)],
        0,
        in_specs=[IN_VMEM] * 2,
        out_specs=[IN_VMEM],
        name="pack_last",
    )(near, partner)
    far, packed = together((far, packed))
    across.append(x_swap(packed))
    total, far = ring(total), ring(far, chips=2)
    *parts, own = local_call(
        near_kernel,
        [two_blocks] * 2 + [(rows, width)],
        9 * block_flops,
        in_specs=[IN_SMEM] + [IN_VMEM] * 3,
        out_specs=[IN_VMEM] * 3,
        name="near_products",
    )(
        jnp.stack([place(step, i) for step in (2, 1) for i in range(X_HI)] + [place(0, 0)]),
        grad,
        *weights,
    )
    terms = [own, jnp.concatenate([across[1][Z + i] for i in range(PARTS)], axis=1)]

    weight_sums = []
    for i in range(PARTS):
        shape = (width // PARTS, features)
        weight_sums += local_call(
            functools.partial(weight_kernel, i),
            [shape],
            16 * block_flops // PARTS,
            in_specs=[IN_SMEM] + [IN_VMEM] * 3,
            out_specs=[IN_VMEM],
            scratch_shapes=[pltpu.VMEM(shape, F32)],
            name="weight_sum",
        )(h[None], near, across[i], grad)
    other_sums = [lax.ppermute(part, "depth", [(0, 1), (1, 0)]) for part in weight_sums]
    total, far, unused = together((total, far, weight_sums[0]))

    (total,) = local_call(
        join_kernel,
        [two_blocks],
        0,
        in_specs=[IN_SMEM] + [IN_VMEM] * 3,
        out_specs=[IN_VMEM],
        name="join_sums",
    )(far_x[None], parts[0], total, far)
    total = ring(total)

    total, unused = together((total, weight_sums[1]))
    last = add(parts[1], total)
    for other_x in range(X_HI):
        terms += [
            ring(last[other_x, :, i * width : (i + 1) * width], other_x, i) for i in range(CORES)
        ]
    terms, other_sums = together((terms, other_sums))
    d_context = sum(t.astype(F32) for t in terms).astype(BF16)
    d_weight = jnp.concatenate([add(*part) for part in zip(weight_sums, other_sums)])
    return (d_context, d_weight)


def solution(mesh):
    in_specs = (P(("depth", "row"), "col"), P(("depth", "col"), "row"), P("col", "row"))
    out_specs = (P(("depth", "row"), "col"), P("col", "row"))
    return jax.shard_map(
        on_device, mesh=mesh, in_specs=in_specs, out_specs=out_specs, check_vma=False
    )
```

```python
import functools

import jax
import jax.numpy as jnp
from jax import lax
from jax.experimental import pallas as pl
from jax.experimental.pallas import tpu as pltpu
from jax.sharding import PartitionSpec as P

X_HI = 2
Z = 8
Y = 8
CORES = 2
PARTS = 2
F32 = jnp.float32
BF16 = jnp.bfloat16
F16 = jnp.float16
POWERS = [12 + 8 * n for n in range(15)]
TAG_ROWS = 16

Z_GROUPS = [[h * Z + z for z in range(Z)] for h in range(X_HI)]
X_SWAP = [(i, (i + Z) % (X_HI * Z)) for i in range(X_HI * Z)]
CORE_SWAP = [(i, i ^ 1) for i in range(Y * CORES)]
IN_VMEM = pl.BlockSpec(memory_space=pltpu.VMEM)
IN_SMEM = pl.BlockSpec(memory_space=pltpu.SMEM)


def scale_kernel(block, out):
    rows = block.shape[0]
    wide = block[...].astype(F32)
    largest = jnp.max(jnp.max(jnp.abs(wide), axis=0, keepdims=True), axis=1, keepdims=True)
    n, scale = jnp.zeros((1, 1), F32), jnp.full((1, 1), 2.0 ** POWERS[0], F32)
    for power in POWERS[1:]:
        small = largest < 2.0 ** (15 - power)
        n = jnp.where(small, n + 1, n)
        scale = jnp.where(small, F32(2.0**power), scale)
    out[:rows] = (wide * scale).astype(BF16)
    out[rows:] = jnp.broadcast_to(n, (TAG_ROWS, block.shape[1])).astype(BF16)


def gather_grad(d_out):
    rows, features = d_out.shape
    (sent,) = local_call(
        scale_kernel,
        [(rows + TAG_ROWS, features)],
        0,
        in_specs=[IN_VMEM],
        out_specs=[IN_VMEM],
        name="scale_block",
    )(d_out)
    return lax.all_gather(sent.astype(F16), "col", axis=0, tiled=True)


def scaled_back(found, rows):
    found = found.reshape(-1, rows + TAG_ROWS, found.shape[1])
    n = found[:, rows, 0].astype(F32)
    back = sum(jnp.where(n == i, F32(2.0**-power), F32(0)) for i, power in enumerate(POWERS))
    return (found[:, :rows].astype(F32) * back[:, None, None]).astype(BF16)


def core_swap(block):
    return lax.ppermute(block, "col", CORE_SWAP)


def x_swap(block):
    return lax.ppermute(block, "row", X_SWAP)


def ring(block, other_x=0, other_core=0, chips=1):
    pairs = []
    for h in range(X_HI):
        for z in range(Z):
            for y in range(Y):
                for k in range(CORES):
                    to_row = (h ^ other_x) * Z + (z + chips * (1 - 2 * k)) % Z
                    source = (h * Z + z) * Y * CORES + y * CORES + k
                    pairs.append((source, to_row * Y * CORES + y * CORES + (k ^ other_core)))
    return lax.ppermute(block, ("row", "col"), pairs)


def local_call(kernel, shapes, flops, **options):
    return pl.pallas_call(
        kernel,
        out_shape=[jax.ShapeDtypeStruct(shape, BF16) for shape in shapes],
        compiler_params=pltpu.CompilerParams(vmem_limit_bytes=40 * 2**20),
        cost_estimate=pl.CostEstimate(flops=flops, bytes_accessed=2**23, transcendentals=0),
        **options,
    )


def dot(grad, weight):
    return lax.dot_general(grad, weight, (((1,), (1,)), ((), ())), preferred_element_type=F32)


def spread_kernel(block, out):
    for i in range(out.shape[0]):
        out[i] = block[...]


def first_kernel(places, here, there, far, partner, weight, other_weight, out, far_out, partner_out):
    rows, width = here.shape[1], weight.shape[0]
    grad = jnp.concatenate([here[0], there[0], far[0], partner[0]])
    found = dot(grad, weight[...]).astype(BF16)
    partner_out[...] = found[3 * rows :]
    for i in range(CORES):
        if i == 1:
            found = dot(grad[: 3 * rows], other_weight[...]).astype(BF16)
        cut = slice(i * width, (i + 1) * width)
        out[0, :, cut] = found[:rows]
        out[1, :, cut] = found[rows : 2 * rows]
        far_out[:, cut] = found[2 * rows : 3 * rows]


def last_kernel(context, partner, out):
    part = out.shape[2]
    out[:Z] = context[:, :, -part:]
    for i in range(PARTS):
        out[Z + i] = partner[:, i * part : (i + 1) * part]


def near_kernel(places, grad, weight, other_weight, *outs):
    *steps, own = outs
    rows, width = grad.shape[1], weight.shape[0]
    for n, out in enumerate(steps):
        both = jnp.concatenate([grad[places[n * X_HI + i]] for i in range(X_HI)])
        for j, w in enumerate((weight, other_weight)):
            found = dot(both, w[...]).astype(BF16)
            for i in range(X_HI):
                out[i, :, j * width : (j + 1) * width] = found[i * rows : (i + 1) * rows]
    own[...] = dot(grad[places[X_HI * len(steps)]], weight[...]).astype(BF16)


def join_kernel(at, part, arrived, far, out):
    other = 1 - at[0]
    total = part[at[0]].astype(F32) + arrived[at[0]].astype(F32) + far[...].astype(F32)
    out[at[0]] = total.astype(BF16)
    out[other] = (part[other].astype(F32) + arrived[other].astype(F32)).astype(BF16)


def weight_kernel(part, x_hi, near, across, grad, out, total):
    width = out.shape[0]
    for other_x, context in enumerate((near, across)):
        cut = slice(part * width, (part + 1) * width) if other_x == 0 else slice(0, width)
        for z in range(0, Z, 2):
            left = jnp.concatenate([context[z + i, :, cut] for i in range(2)])
            at = (x_hi[0] ^ other_x) * Z + z
            right = jnp.concatenate([grad[at + i] for i in range(2)])
            term = lax.dot_general(left, right, (((0,), (0,)), ((), ())), preferred_element_type=F32)
            if other_x == 0 and z == 0:
                total[...] = term
            else:
                total[...] += term
    out[...] = total[...].astype(BF16)


def on_device(context, d_out, out_weight):
    rows, features = d_out.shape
    width = out_weight.shape[0]
    row, col = lax.axis_index("row"), lax.axis_index("col")
    h, z = row // Z, row % Z
    core = col % CORES
    together = lax.optimization_barrier

    (spread,) = local_call(
        spread_kernel,
        [(Z, rows, width)],
        0,
        in_specs=[IN_VMEM],
        out_specs=[IN_VMEM],
        name="spread_context",
    )(context)
    near = lax.all_to_all(spread, "row", 0, 0, tiled=True, axis_index_groups=Z_GROUPS)
    found, out_weight = together((gather_grad(d_out), out_weight))
    weights = (out_weight, core_swap(out_weight))
    grad, near = together((scaled_back(found, rows), near))
    part = width // PARTS
    packed = near[:, :, :part]
    grad, packed = together((grad, packed))
    across = [x_swap(packed)]

    def place(step, other_x):
        return (h ^ other_x) * Z + (z + (1 - 2 * core) * step + Z) % Z

    def add(a, b):
        return (a.astype(F32) + b.astype(F32)).astype(BF16)

    block_flops = 2 * rows * features * width
    two_blocks = (X_HI, rows, CORES * width)
    far_x = h ^ core
    total, far, partner = local_call(
        first_kernel,
        [two_blocks, two_blocks[1:], (rows, width)],
        7 * block_flops,
        grid_spec=pltpu.PrefetchScalarGridSpec(
            num_scalar_prefetch=1,
            grid=(1,),
            in_specs=[
                pl.BlockSpec((1, rows, features), lambda i, places, n=n: (places[n], 0, 0))
                for n in range(4)
            ]
            + [IN_VMEM] * 2,
            out_specs=[IN_VMEM] * 3,
        ),
        name="first_products",
    )(
        jnp.stack([place(3, 0), place(3, 1), place(4, far_x), place(0, 1)]), *[grad] * 4, *weights
    )
    (packed,) = local_call(
        last_kernel,
        [(Z + PARTS, rows, part)],
        0,
        in_specs=[IN_VMEM] * 2,
        out_specs=[IN_VMEM],
        name="pack_last",
    )(near, partner)
    far, packed = together((far, packed))
    across.append(x_swap(packed))
    total, far = ring(total), ring(far, chips=2)
    *parts, own = local_call(
        near_kernel,
        [two_blocks] * 2 + [(rows, width)],
        9 * block_flops,
        in_specs=[IN_SMEM] + [IN_VMEM] * 3,
        out_specs=[IN_VMEM] * 3,
        name="near_products",
    )(
        jnp.stack([place(step, i) for step in (2, 1) for i in range(X_HI)] + [place(0, 0)]),
        grad,
        *weights,
    )
    terms = [own, jnp.concatenate([across[1][Z + i] for i in range(PARTS)], axis=1)]

    weight_sums = []
    for i in range(PARTS):
        shape = (width // PARTS, features)
        weight_sums += local_call(
            functools.partial(weight_kernel, i),
            [shape],
            16 * block_flops // PARTS,
            in_specs=[IN_SMEM] + [IN_VMEM] * 3,
            out_specs=[IN_VMEM],
            scratch_shapes=[pltpu.VMEM(shape, F32)],
            name="weight_sum",
        )(h[None], near, across[i], grad)
    other_sums = [lax.ppermute(part, "depth", [(0, 1), (1, 0)]) for part in weight_sums]
    total, far, unused = together((total, far, weight_sums[0]))

    (total,) = local_call(
        join_kernel,
        [two_blocks],
        0,
        in_specs=[IN_SMEM] + [IN_VMEM] * 3,
        out_specs=[IN_VMEM],
        name="join_sums",
    )(far_x[None], parts[0], total, far)
    total = ring(total)

    total, unused = together((total, weight_sums[1]))
    last = add(parts[1], total)
    for other_x in range(X_HI):
        terms += [
            ring(last[other_x, :, i * width : (i + 1) * width], other_x, i) for i in range(CORES)
        ]
    d_weight = lax.dynamic_update_slice(
        jnp.zeros((width, features), BF16), add(weight_sums[0], other_sums[0]), (0, 0)
    )
    terms, late, d_weight = together((terms, other_sums[1], d_weight))
    d_context = sum(t.astype(F32) for t in terms).astype(BF16)
    d_weight = lax.dynamic_update_slice(d_weight, add(weight_sums[1], late), (part, 0))
    return (d_context, d_weight)


def solution(mesh):
    in_specs = (P(("depth", "row"), "col"), P(("depth", "col"), "row"), P("col", "row"))
    out_specs = (P(("depth", "row"), "col"), P("col", "row"))
    return jax.shard_map(
        on_device, mesh=mesh, in_specs=in_specs, out_specs=out_specs, check_vma=False
    )
```

```python
import functools

import jax
import jax.numpy as jnp
from jax import lax
from jax.experimental import pallas as pl
from jax.experimental.pallas import tpu as pltpu
from jax.sharding import PartitionSpec as P

X_HI = 2
Z = 8
Y = 8
CORES = 2
PARTS = 2
F32 = jnp.float32
BF16 = jnp.bfloat16
F16 = jnp.float16
POWERS = [12 + 8 * n for n in range(15)]
TAG_ROWS = 16

Z_GROUPS = [[h * Z + z for z in range(Z)] for h in range(X_HI)]
X_SWAP = [(i, (i + Z) % (X_HI * Z)) for i in range(X_HI * Z)]
CORE_SWAP = [(i, i ^ 1) for i in range(Y * CORES)]
IN_VMEM = pl.BlockSpec(memory_space=pltpu.VMEM)
IN_SMEM = pl.BlockSpec(memory_space=pltpu.SMEM)


def scale_kernel(block, out):
    rows = block.shape[0]
    wide = block[...].astype(F32)
    largest = jnp.max(jnp.max(jnp.abs(wide), axis=0, keepdims=True), axis=1, keepdims=True)
    n, scale = jnp.zeros((1, 1), F32), jnp.full((1, 1), 2.0 ** POWERS[0], F32)
    for power in POWERS[1:]:
        small = largest < 2.0 ** (15 - power)
        n = jnp.where(small, n + 1, n)
        scale = jnp.where(small, F32(2.0**power), scale)
    out[:rows] = (wide * scale).astype(BF16)
    out[rows:] = jnp.broadcast_to(n, (TAG_ROWS, block.shape[1])).astype(BF16)


def gather_grad(d_out):
    rows, features = d_out.shape
    (sent,) = local_call(
        scale_kernel,
        [(rows + TAG_ROWS, features)],
        0,
        in_specs=[IN_VMEM],
        out_specs=[IN_VMEM],
        name="scale_block",
    )(d_out)
    return lax.all_gather(sent.astype(F16), "col", axis=0, tiled=True)


def scaled_back(found, rows):
    found = found.reshape(-1, rows + TAG_ROWS, found.shape[1])
    n = found[:, rows, 0].astype(F32)
    back = sum(jnp.where(n == i, F32(2.0**-power), F32(0)) for i, power in enumerate(POWERS))
    return (found[:, :rows].astype(F32) * back[:, None, None]).astype(BF16)


def core_swap(block):
    return lax.ppermute(block, "col", CORE_SWAP)


def x_swap(block):
    return lax.ppermute(block, "row", X_SWAP)


def ring(block, other_x=0, other_core=0, chips=1):
    pairs = []
    for h in range(X_HI):
        for z in range(Z):
            for y in range(Y):
                for k in range(CORES):
                    to_row = (h ^ other_x) * Z + (z + chips * (1 - 2 * k)) % Z
                    source = (h * Z + z) * Y * CORES + y * CORES + k
                    pairs.append((source, to_row * Y * CORES + y * CORES + (k ^ other_core)))
    return lax.ppermute(block, ("row", "col"), pairs)


def local_call(kernel, shapes, flops, **options):
    return pl.pallas_call(
        kernel,
        out_shape=[jax.ShapeDtypeStruct(shape, BF16) for shape in shapes],
        compiler_params=pltpu.CompilerParams(vmem_limit_bytes=40 * 2**20),
        cost_estimate=pl.CostEstimate(flops=flops, bytes_accessed=2**23, transcendentals=0),
        **options,
    )


def dot(grad, weight):
    return lax.dot_general(grad, weight, (((1,), (1,)), ((), ())), preferred_element_type=F32)


def spread_kernel(block, out):
    for i in range(out.shape[0]):
        out[i] = block[...]


def first_kernel(places, here, there, far, partner, weight, other_weight, out, far_out, partner_out):
    rows, width = here.shape[1], weight.shape[0]
    grad = jnp.concatenate([here[0], there[0], far[0], partner[0]])
    found = dot(grad, weight[...]).astype(BF16)
    partner_out[...] = found[3 * rows :]
    for i in range(CORES):
        if i == 1:
            found = dot(grad[: 3 * rows], other_weight[...]).astype(BF16)
        cut = slice(i * width, (i + 1) * width)
        out[0, :, cut] = found[:rows]
        out[1, :, cut] = found[rows : 2 * rows]
        far_out[:, cut] = found[2 * rows : 3 * rows]


def last_kernel(context, partner, out):
    part = out.shape[2]
    out[:Z] = context[...]
    for i in range(PARTS):
        out[Z + i] = partner[:, i * part : (i + 1) * part]


def near_kernel(places, grad, weight, other_weight, *outs):
    *steps, own = outs
    rows, width = grad.shape[1], weight.shape[0]
    for n, out in enumerate(steps):
        both = jnp.concatenate([grad[places[n * X_HI + i]] for i in range(X_HI)])
        for j, w in enumerate((weight, other_weight)):
            found = dot(both, w[...]).astype(BF16)
            for i in range(X_HI):
                out[i, :, j * width : (j + 1) * width] = found[i * rows : (i + 1) * rows]
    own[...] = dot(grad[places[X_HI * len(steps)]], weight[...]).astype(BF16)


def join_kernel(at, part, arrived, far, out):
    other = 1 - at[0]
    total = part[at[0]].astype(F32) + arrived[at[0]].astype(F32) + far[...].astype(F32)
    out[at[0]] = total.astype(BF16)
    out[other] = (part[other].astype(F32) + arrived[other].astype(F32)).astype(BF16)


def weight_kernel(part, x_hi, near, across, grad, out, total):
    width = out.shape[0]
    for other_x, context in enumerate((near, across)):
        cut = slice(part * width, (part + 1) * width) if other_x == 0 else slice(0, width)
        for z in range(0, Z, 2):
            left = jnp.concatenate([context[z + i, :, cut] for i in range(2)])
            at = (x_hi[0] ^ other_x) * Z + z
            right = jnp.concatenate([grad[at + i] for i in range(2)])
            term = lax.dot_general(left, right, (((0,), (0,)), ((), ())), preferred_element_type=F32)
            if other_x == 0 and z == 0:
                total[...] = term
            else:
                total[...] += term
    out[...] = total[...].astype(BF16)


def on_device(context, d_out, out_weight):
    rows, features = d_out.shape
    width = out_weight.shape[0]
    row, col = lax.axis_index("row"), lax.axis_index("col")
    h, z = row // Z, row % Z
    core = col % CORES
    together = lax.optimization_barrier

    (spread,) = local_call(
        spread_kernel,
        [(Z, rows, width)],
        0,
        in_specs=[IN_VMEM],
        out_specs=[IN_VMEM],
        name="spread_context",
    )(context)
    near = lax.all_to_all(spread, "row", 0, 0, tiled=True, axis_index_groups=Z_GROUPS)
    found, out_weight = together((gather_grad(d_out), out_weight))
    weights = (out_weight, core_swap(out_weight))
    grad, near = together((scaled_back(found, rows), near))
    part = width // PARTS
    packed = near[:, :, :part]
    grad, packed = together((grad, packed))
    across = [x_swap(packed)]

    def place(step, other_x):
        return (h ^ other_x) * Z + (z + (1 - 2 * core) * step + Z) % Z

    def add(a, b):
        return (a.astype(F32) + b.astype(F32)).astype(BF16)

    block_flops = 2 * rows * features * width
    two_blocks = (X_HI, rows, CORES * width)
    far_x = h ^ core
    total, far, partner = local_call(
        first_kernel,
        [two_blocks, two_blocks[1:], (rows, width)],
        7 * block_flops,
        grid_spec=pltpu.PrefetchScalarGridSpec(
            num_scalar_prefetch=1,
            grid=(1,),
            in_specs=[
                pl.BlockSpec((1, rows, features), lambda i, places, n=n: (places[n], 0, 0))
                for n in range(4)
            ]
            + [IN_VMEM] * 2,
            out_specs=[IN_VMEM] * 3,
        ),
        name="first_products",
    )(
        jnp.stack([place(3, 0), place(3, 1), place(4, far_x), place(0, 1)]), *[grad] * 4, *weights
    )
    (packed,) = local_call(
        last_kernel,
        [(Z + PARTS, rows, part)],
        0,
        grid=(1,),
        in_specs=[
            pl.BlockSpec((Z, rows, part), lambda i: (0, 0, PARTS - 1)),
            pl.BlockSpec((rows, width), lambda i: (0, 0)),
        ],
        out_specs=[pl.BlockSpec((Z + PARTS, rows, part), lambda i: (0, 0, 0))],
        name="pack_last",
    )(near, partner)
    far, packed = together((far, packed))
    across.append(x_swap(packed))
    total, far = ring(total), ring(far, chips=2)
    *parts, own = local_call(
        near_kernel,
        [two_blocks] * 2 + [(rows, width)],
        9 * block_flops,
        in_specs=[IN_SMEM] + [IN_VMEM] * 3,
        out_specs=[IN_VMEM] * 3,
        name="near_products",
    )(
        jnp.stack([place(step, i) for step in (2, 1) for i in range(X_HI)] + [place(0, 0)]),
        grad,
        *weights,
    )
    terms = [own, jnp.concatenate([across[1][Z + i] for i in range(PARTS)], axis=1)]

    weight_sums = []
    for i in range(PARTS):
        shape = (width // PARTS, features)
        weight_sums += local_call(
            functools.partial(weight_kernel, i),
            [shape],
            16 * block_flops // PARTS,
            in_specs=[IN_SMEM] + [IN_VMEM] * 3,
            out_specs=[IN_VMEM],
            scratch_shapes=[pltpu.VMEM(shape, F32)],
            name="weight_sum",
        )(h[None], near, across[i], grad)
    other_sums = [lax.ppermute(part, "depth", [(0, 1), (1, 0)]) for part in weight_sums]
    total, far, unused = together((total, far, weight_sums[0]))

    (total,) = local_call(
        join_kernel,
        [two_blocks],
        0,
        in_specs=[IN_SMEM] + [IN_VMEM] * 3,
        out_specs=[IN_VMEM],
        name="join_sums",
    )(far_x[None], parts[0], total, far)
    total = ring(total)

    total, unused = together((total, weight_sums[1]))
    last = add(parts[1], total)
    for other_x in range(X_HI):
        terms += [
            ring(last[other_x, :, i * width : (i + 1) * width], other_x, i) for i in range(CORES)
        ]
    d_weight = lax.dynamic_update_slice(
        jnp.zeros((width, features), BF16), add(weight_sums[0], other_sums[0]), (0, 0)
    )
    terms, late, d_weight = together((terms, other_sums[1], d_weight))
    d_context = sum(t.astype(F32) for t in terms).astype(BF16)
    d_weight = lax.dynamic_update_slice(d_weight, add(weight_sums[1], late), (part, 0))
    return (d_context, d_weight)


def solution(mesh):
    in_specs = (P(("depth", "row"), "col"), P(("depth", "col"), "row"), P("col", "row"))
    out_specs = (P(("depth", "row"), "col"), P("col", "row"))
    return jax.shard_map(
        on_device, mesh=mesh, in_specs=in_specs, out_specs=out_specs, check_vma=False
    )
```
